32 devices in a mesh: replica: 2 (over y), adapter: 4 (over z), tensor: 4 (over x, core).
Axes of the slice: x: 2, y: 2, z: 4, core: 2. Of those that a mesh axis runs over, the one named last changes fastest.
Arguments:
- hidden: bfloat16 [512, 4, 8192], P(('replica', 'adapter'), None, 'tensor'), parts along dimension 0, may hold values from -6 to 6
- unrotated_queries: bfloat16 [512, 4, 8192], P(('replica', 'adapter'), None, 'tensor'), parts along dimension 0, may hold values from -6 to 6
- adapter_ids: int32 [512], P(('replica', 'adapter')), parts along dimension 0, may hold values from 0 to 31, as said below
- adapter_home: int32 [64], P('replica'), parts along dimension 0, may hold values from 0 to 31, as said below
- reduce_matrices: bfloat16 [32, 8192, 64], P('adapter', 'tensor'), may hold values from -0.0625 to 0.0625
- expand_matrices: bfloat16 [32, 64, 8192], P('adapter', None, 'tensor'), may hold values from -0.75 to 0.75
- correction_gain_table: float32 [32], P('adapter'), may hold values from 0.25 to 2
- key_cache: bfloat16 [512, 8, 128, 128], P(('replica', 'adapter'), 'tensor'), parts along dimension 0, may hold values from -400 to 400
- value_cache: bfloat16 [512, 8, 128, 128], P(('replica', 'adapter'), 'tensor'), parts along dimension 0, may hold values from -6 to 6
- new_keys: bfloat16 [512, 4, 8, 128], P(('replica', 'adapter'), None, 'tensor'), parts along dimension 0, may hold values from -6 to 6
- new_values: bfloat16 [512, 4, 8, 128], P(('replica', 'adapter'), None, 'tensor'), parts along dimension 0, may hold values from -6 to 6
- cache_len: int32 [512], P(('replica', 'adapter')), parts along dimension 0, may hold values from 2 to 128
Outputs:
- attended: bfloat16 [512, 4, 8192], P(('replica', 'adapter'), None, 'tensor'), parts along dimension 0
The draws below stay inside these ranges and needn't reach their ends.
There are 2 independent parts, one for each index of `replica`. The reference program is written for one: setup_inputs(seed, part) draws one part's arguments, and reference() takes and returns one part's arrays. A program takes and returns all parts, laid end to end along the dimension named above; an argument that names none is the same for every part. Nothing has to cross between parts.
Inputs may be any that keep to these rules, and one draw needn't show every extreme that they name: `adapter_ids`: of the 64 requests of one index of adapter, at most 32 use adapters homed on any one index, and in every draw some index receives exactly 32 from every index. `adapter_home`: A permutation from adapter to home slot; slot s lies on index s // 8 of adapter, at its local slot s % 8.
All inputs are finite; a program needn't handle non-finite values.
Results may differ from the reference program's by a relative error of at most 0.0093.
Values may be sent and summed in bfloat16 or wider, within the bound.
A program may use at most 128 MiB of HBM per device.

```python
import math
import jax
import jax.numpy as jnp
from jax import lax

D = 8192
HEADS = 64
KV_HEADS = 8
HEAD_DIM = 128
RANK = 64
POS = 4
REQ_DEV = 64
ADAPT_DEV = 8
CONTEXT = 128
REQUESTS = 256
ADAPTERS = 32
CAP = 32
HOT = 1
N_ADAPTER = 4


def routing_tables(base_key):
    keys_list = jax.random.split(base_key, 5)
    slot_total = N_ADAPTER * CAP
    hot_order = jax.random.permutation(keys_list[0], N_ADAPTER)
    slot_device = jnp.arange(slot_total, dtype=jnp.int32) // CAP
    is_hot = jnp.any(slot_device[:, None] == hot_order[None, :HOT], axis=1)
    noise_bits = jax.random.randint(keys_list[1], (N_ADAPTER, slot_total), 0, 1 << 16)
    scores = noise_bits * slot_total + jnp.arange(slot_total, dtype=jnp.int32)[None, :] + jnp.where(is_hot, 1 << 27, 0)[None, :]
    chosen = lax.top_k(scores, REQ_DEV)[1]
    shuffled = jax.vmap(jax.random.permutation)(jax.random.split(keys_list[2], N_ADAPTER), chosen)
    local_slot = jax.random.randint(keys_list[3], (N_ADAPTER, REQ_DEV), 0, ADAPT_DEV)
    home_slot = shuffled // CAP * ADAPT_DEV + local_slot
    placement = jax.random.permutation(keys_list[4], ADAPTERS).astype(jnp.int32)
    inverse = jnp.argsort(placement)
    return (jnp.take(inverse, home_slot.reshape(-1)).astype(jnp.int32), placement)


def draw_adapter_ids(key, part):
    return routing_tables(key)[0]


def draw_adapter_home(key, part):
    return routing_tables(key)[1]


def draw_cache_len(key, part):
    key = jax.random.fold_in(key, 5)
    keys_list = jax.random.split(key, 3)
    factor = jax.random.randint(keys_list[0], (N_ADAPTER, 1), 1, 5)
    lengths = 2 + jax.random.randint(keys_list[1], (N_ADAPTER, REQ_DEV), 0, CONTEXT - 1) * factor // 4
    longest = jax.random.randint(keys_list[2], (N_ADAPTER, 1), 0, REQ_DEV)
    lengths = jnp.where(jnp.arange(REQ_DEV, dtype=jnp.int32)[None, :] == longest, CONTEXT, lengths)
    return lengths.reshape(-1).astype(jnp.int32)


def draw_key_cache(key, part):
    key = jax.random.fold_in(key, 11)
    keys_list = jax.random.split(key, 1)
    shape_full = (REQUESTS, KV_HEADS, CONTEXT, HEAD_DIM)
    values = jnp.clip(jax.random.normal(keys_list[0], shape_full, jnp.float32), -6.0, 6.0)
    return values.astype(jnp.bfloat16)


def shard_levels(stream_key, shape, cuts, least, top_value):
    loudness, own = 1.0, jax.random.fold_in(stream_key, 6)
    for dim, parts in cuts:
        steps = jnp.exp(jax.random.uniform(jax.random.fold_in(own, dim), (parts,), jnp.float32, least / len(cuts), top_value / len(cuts)))
        loudness = loudness * jnp.repeat(steps, shape[dim] // parts).reshape([-1 if axis == dim else 1 for axis in range(len(shape))])
    return loudness


def bell_draw(own_key, shape, scale, limit, cuts=(), kind=jnp.bfloat16):
    values = jax.random.normal(own_key, shape, jnp.float32) * scale
    if len(cuts) > 0:
        values = shard_levels(own_key, shape, cuts, -0.22, 0.18) * values
    return jnp.clip(values, min=-limit, max=limit).astype(kind)


def setup_inputs(seed: int = 0, part: int = 0) -> dict:
    seeds = jax.random.split(jax.random.key(seed), 13)
    part_splits = jax.random.split(jax.random.fold_in(seeds[12], part), 13)
    hidden = bell_draw(part_splits[0], (REQUESTS, POS, D), 1.0, 6.0, ((0, 4), (2, 4)))
    unrotated_queries = bell_draw(part_splits[1], (REQUESTS, POS, D), 1.0, 6.0, ((0, 4), (2, 4)))
    adapter_ids = draw_adapter_ids(jax.random.fold_in(jax.random.fold_in(seeds[12], part), 71), part)
    adapter_home = draw_adapter_home(jax.random.fold_in(jax.random.fold_in(seeds[12], part), 71), part)
    reduce_matrices = bell_draw(seeds[4], (ADAPTERS, D, RANK), D ** -0.5, 0.0625, ((0, 4), (1, 4)))
    expand_matrices = bell_draw(seeds[5], (ADAPTERS, RANK, D), RANK ** -0.5, 0.75, ((0, 4), (2, 4)))
    correction_gain_table = jnp.clip(jnp.exp(math.log(2.0) - 2.0794415 * jax.random.uniform(seeds[6], (ADAPTERS,), jnp.float32) ** shard_levels(seeds[6], (ADAPTERS,), ((0, 4),), -0.2, 0.2)), 0.25, 2.0)
    key_cache = draw_key_cache(jax.random.fold_in(jax.random.fold_in(seeds[12], part), 71), part)
    value_cache = bell_draw(part_splits[8], (REQUESTS, KV_HEADS, CONTEXT, HEAD_DIM), 1.0, 6.0, ((0, 4), (1, 4)))
    new_keys = bell_draw(part_splits[9], (REQUESTS, POS, KV_HEADS, HEAD_DIM), 1.0, 6.0, ((0, 4), (2, 4)))
    new_values = bell_draw(part_splits[10], (REQUESTS, POS, KV_HEADS, HEAD_DIM), 1.0, 6.0, ((0, 4), (2, 4)))
    cache_len = draw_cache_len(jax.random.fold_in(jax.random.fold_in(seeds[12], part), 71), part)
    return dict(hidden=hidden, unrotated_queries=unrotated_queries, adapter_ids=adapter_ids, adapter_home=adapter_home, reduce_matrices=reduce_matrices, expand_matrices=expand_matrices, correction_gain_table=correction_gain_table, key_cache=key_cache, value_cache=value_cache, new_keys=new_keys, new_values=new_values, cache_len=cache_len)


rope_theta = 500000.0


def rotate(query, lengths):
    head_dim = query.shape[-1]
    half_dim = head_dim // 2
    frequency = rope_theta ** (-2.0 * jnp.arange(half_dim, dtype=jnp.float32) / head_dim)
    offsets = lengths[:, None] + jnp.arange(query.shape[1], dtype=jnp.int32)[None, :]
    angles = offsets.astype(jnp.float32)[:, :, None] * frequency[None, None, :]
    cos_part = jnp.concatenate([jnp.cos(angles), jnp.cos(angles)], axis=-1)[:, :, None, :]
    sin_part = jnp.concatenate([jnp.sin(angles), jnp.sin(angles)], axis=-1)[:, :, None, :]
    turned = jnp.concatenate([-query[..., half_dim:], query[..., :half_dim]], axis=-1)
    return query * cos_part + turned * sin_part


def attend(query, key_block, value_block, fresh_keys, fresh_values, lengths):
    batch_size, iteration_total, head_count, head_dim = query.shape
    kv_local = key_block.shape[1]
    context = key_block.shape[2]
    grouped = query.reshape(batch_size, iteration_total, kv_local, head_count // kv_local, head_dim).astype(jnp.float32)
    scaling = head_dim ** -0.5
    old_scores = jnp.einsum("bpkgd,bktd->bpkgt", grouped, key_block.astype(jnp.float32)) * scaling
    new_scores = jnp.einsum("bpkgd,bqkd->bpkgq", grouped, fresh_keys.astype(jnp.float32)) * scaling
    old_valid = (jnp.arange(context, dtype=jnp.int32)[None, :] < lengths[:, None])[:, None, None, None, :]
    new_valid = (jnp.arange(iteration_total)[None, :] <= jnp.arange(iteration_total)[:, None])[None, :, None, None, :]
    old_scores = jnp.where(old_valid, old_scores, -jnp.inf)
    new_scores = jnp.where(new_valid, new_scores, -jnp.inf)
    row_top = jnp.maximum(jnp.max(old_scores, axis=-1, keepdims=True), jnp.max(new_scores, axis=-1, keepdims=True))
    old_exp = jnp.exp(old_scores - row_top)
    new_exp = jnp.exp(new_scores - row_top)
    row_total = jnp.sum(old_exp, axis=-1, keepdims=True) + jnp.sum(new_exp, axis=-1, keepdims=True)
    old_weights = (old_exp / row_total).astype(jnp.bfloat16)
    new_weights = (new_exp / row_total).astype(jnp.bfloat16)
    accumulated_total = jnp.einsum("bpkgt,bktd->bpkgd", old_weights.astype(jnp.float32), value_block.astype(jnp.float32))
    accumulated_total = accumulated_total + jnp.einsum("bpkgq,bqkd->bpkgd", new_weights.astype(jnp.float32), fresh_values.astype(jnp.float32))
    return accumulated_total.reshape(batch_size, iteration_total, head_count * head_dim).astype(jnp.bfloat16)


def low_rank_piece(request_group, resident_position_list, reduce_matrices, expand_matrices, correction_gain_table):
    down_part = jnp.take(reduce_matrices, resident_position_list, axis=0).astype(jnp.float32)
    shrunk = jnp.einsum("bpd,bdr->bpr", request_group.astype(jnp.float32), down_part)
    scales = jnp.take(correction_gain_table, resident_position_list)
    shrunk = (shrunk * scales[:, None, None]).astype(jnp.bfloat16)
    up_part = jnp.take(expand_matrices, resident_position_list, axis=0).astype(jnp.float32)
    return jnp.einsum("bpr,brd->bpd", shrunk.astype(jnp.float32), up_part).astype(jnp.bfloat16)


def reference(hidden, unrotated_queries, adapter_ids, adapter_home, reduce_matrices, expand_matrices, correction_gain_table, key_cache, value_cache, new_keys, new_values, cache_len):
    home_slot = jnp.take(adapter_home, adapter_ids).astype(jnp.int32)
    block_size = math.gcd(REQUESTS, 32)
    block_count = REQUESTS // block_size

    def split_rows(array):
        return array.reshape((block_count, block_size) + array.shape[1:])

    def one_block(pieces):
        request_group, shared_projection_piece, resident_position_list, key_block, value_block, fresh_keys, fresh_values, lengths = pieces
        low_rank_correction = low_rank_piece(request_group, resident_position_list, reduce_matrices, expand_matrices, correction_gain_table)
        accumulated_total = shared_projection_piece.astype(jnp.float32) + low_rank_correction.astype(jnp.float32)
        query = rotate(accumulated_total.reshape(block_size, POS, HEADS, HEAD_DIM), lengths).astype(jnp.bfloat16)
        return attend(query, key_block, value_block, fresh_keys, fresh_values, lengths)

    inputs = tuple(split_rows(array) for array in (hidden, unrotated_queries, home_slot, key_cache, value_cache, new_keys, new_values, cache_len))
    outputs = lax.map(one_block, inputs)
    return outputs.reshape(REQUESTS, POS, D)
```

```python
import functools

import jax
import jax.numpy as jnp
from jax import lax
from jax.experimental import pallas as pl
from jax.experimental.pallas import tpu as pltpu
from jax.sharding import PartitionSpec as P

rope_theta = 500000.0
MESH = pl.DeviceIdType.MESH


def nt_dot(a, b):
    return lax.dot_general(a, b, (((1,), (1,)), ((), ())), preferred_element_type=jnp.float32)


def log2(n):
    bits = n.bit_length() - 1
    assert 1 << bits == n
    return bits


def kernel(
    dims,
    len_ref,
    pos_ref,
    pos_col_ref,
    slot_ref,
    gain_ref,
    hidden_hbm,
    uq_hbm,
    down_hbm,
    up_hbm,
    key_hbm,
    value_hbm,
    fresh_key_hbm,
    fresh_value_hbm,
    cos_ref,
    sin_ref,
    out_ref,
    hidden,
    uq,
    down,
    up,
    keys,
    values,
    outgoing,
    arrived,
    labels_out,
    labels_in,
    partial,
    returning,
    returned,
    rows,
    local_sems,
    out_send,
    out_recv,
    label_send,
    label_recv,
    part_send,
    part_recv,
    back_send,
    back_recv,
):
    n, tensors, chunks, cap, reqs, positions, context = dims
    per = positions // chunks
    block = per * cap
    total = n * block
    half = total // 2
    width = hidden.shape[-1]
    heads = width // 128
    kv = keys.shape[1]
    group = heads // kv
    row_count = positions * heads
    replica = lax.axis_index("replica")
    me = lax.axis_index("adapter")
    column = lax.axis_index("tensor")

    def adapter_peer(k):
        return (replica, lax.rem(me + k + n, n), column)

    def tensor_peer(k):
        return (replica, me, lax.rem(column + k, tensors))

    loads = [
        pltpu.make_async_copy(hidden_hbm, hidden, local_sems.at[0]),
        pltpu.make_async_copy(down_hbm, down, local_sems.at[1]),
        pltpu.make_async_copy(up_hbm, up, local_sems.at[2]),
        pltpu.make_async_copy(uq_hbm, uq, local_sems.at[3]),
        pltpu.make_async_copy(key_hbm, keys.at[:, :, pl.ds(0, context), :], local_sems.at[4]),
        pltpu.make_async_copy(value_hbm, values.at[:, :, pl.ds(0, context), :], local_sems.at[5]),
        pltpu.make_async_copy(
            fresh_key_hbm, keys.at[:, :, pl.ds(context, 16), :], local_sems.at[6]
        ),
        pltpu.make_async_copy(
            fresh_value_hbm, values.at[:, :, pl.ds(context, 16), :], local_sems.at[7]
        ),
    ]
    for load in loads:
        load.start()

    barrier = pltpu.get_barrier_semaphore()
    for k in range(1, n):
        pl.semaphore_signal(barrier, inc=1, device_id=adapter_peer(k), device_id_type=MESH)
    for k in range(1, tensors):
        pl.semaphore_signal(barrier, inc=1, device_id=tensor_peer(k), device_id_type=MESH)

    def out_copy(c, k):
        return pltpu.make_async_remote_copy(
            outgoing.at[c, k], arrived.at[c, k], out_send.at[c, k], out_recv.at[c, k],
            device_id=adapter_peer(k), device_id_type=MESH,
        )

    def label_copy(k):
        return pltpu.make_async_remote_copy(
            labels_out.at[k], labels_in.at[k], label_send.at[k], label_recv.at[k],
            device_id=adapter_peer(k), device_id_type=MESH,
        )

    def part_copy(c, k):
        return pltpu.make_async_remote_copy(
            partial.at[c, 0], partial.at[c, k], part_send.at[c, k], part_recv.at[c, k],
            device_id=tensor_peer(k), device_id_type=MESH,
        )

    def back_copy(c, k):
        return pltpu.make_async_remote_copy(
            returning.at[c, k], returned.at[c, k], back_send.at[c, k], back_recv.at[c, k],
            device_id=adapter_peer(-k), device_id_type=MESH,
        )

    def pick(shape, row_axis, pos):
        row = lax.broadcasted_iota(jnp.int32, shape, row_axis)
        col = lax.broadcasted_iota(jnp.int32, shape, 1 - row_axis)
        peer = row >> log2(block)
        row_pos = (row >> log2(cap)) & (per - 1)
        slot = row & (cap - 1)
        return (pos == peer * cap + slot) & (row_pos == (col >> log2(reqs)))

    forward = pick((total, per * reqs), 0, pos_ref[...])
    label_rows = jnp.sum(jnp.where(forward, slot_ref[...], 0), axis=1, keepdims=True)
    label_rows = jnp.broadcast_to(label_rows, (total, 128)).reshape(n, block, 128)
    labels_out[...] = label_rows
    labels_in[0] = label_rows[0]
    forward = jnp.where(forward, 1.0, 0.0).astype(jnp.bfloat16)

    loads[0].wait()
    pl.semaphore_wait(barrier, n - 1 + tensors - 1)
    for k in range(1, n):
        label_copy(k).start()

    def dispatch(c, _):
        source = hidden[pl.ds(pl.multiple_of(c * per * reqs, per * reqs), per * reqs), :]
        sent = jnp.dot(forward, source, preferred_element_type=jnp.float32)
        sent = sent.astype(jnp.bfloat16).reshape(n, block, width)
        outgoing[c] = sent
        arrived[c, 0] = sent[0]
        for k in range(1, n):
            out_copy(c, k).start()
        return 0

    lax.fori_loop(0, chunks, dispatch, 0)
    for k in range(1, n):
        label_copy(k).wait()
    loads[1].wait()
    loads[2].wait()

    def work(c, _):
        for k in range(1, n):
            out_copy(c, k).wait_recv()
        label = labels_in[...].reshape(total, 128)
        lane = lax.broadcasted_iota(jnp.int32, (total, 128), 1)
        odd = jnp.where(lane >= 64, 1, 0)
        product = nt_dot(arrived[c].reshape(total, width), down[...])
        kept = jnp.zeros((total, 128), jnp.float32)
        groups = down.shape[0] // 128
        for j in range(groups):
            kept = kept + jnp.where(label == 2 * j + odd, product[:, j * 128 : (j + 1) * 128], 0.0)
        kept = kept + pltpu.roll(kept, 64, 1)
        low = lax.broadcasted_iota(jnp.int32, (half, 128), 1) < 64
        partial[c, 0] = jnp.where(low, kept[:half], kept[half:])
        for k in range(1, tensors):
            part_copy(c, k).start()
        for k in range(1, tensors):
            part_copy(c, k).wait()
        summed = partial[c, 0]
        for k in range(1, tensors):
            summed = summed + partial[c, k]
        turned = pltpu.roll(summed, 64, 1)
        both = jnp.concatenate(
            [jnp.where(low, summed, turned), jnp.where(low, turned, summed)], axis=0
        )
        pieces = []
        for j in range(groups):
            scaled = both * gain_ref[:, j * 128 : (j + 1) * 128]
            pieces.append(jnp.where(label == 2 * j + odd, scaled, 0.0).astype(jnp.bfloat16))
        shrunk = jnp.concatenate(pieces, axis=1)
        expanded = jnp.dot(shrunk, up[...], preferred_element_type=jnp.float32)
        expanded = expanded.astype(jnp.bfloat16).reshape(n, block, width)
        returning[c] = expanded
        returned[c, 0] = expanded[0]
        for k in range(1, n):
            back_copy(c, k).start()
        return 0

    lax.fori_loop(0, chunks, work, 0)

    backward = pick((per * reqs, total), 1, pos_col_ref[...])
    backward = jnp.where(backward, 1.0, 0.0).astype(jnp.bfloat16)
    loads[3].wait()

    def combine(c, _):
        for k in range(1, n):
            back_copy(c, k).wait_recv()
        span = pl.ds(pl.multiple_of(c * per * reqs, per * reqs), per * reqs)
        delta = jnp.dot(
            backward, returned[c].reshape(total, width), preferred_element_type=jnp.float32
        )
        merged = uq[span, :].astype(jnp.float32) + delta
        cosine = cos_ref[span, :]
        sine = sin_ref[span, :]
        for h in range(heads):
            part = merged[:, h * 128 : (h + 1) * 128]
            part = part * cosine + pltpu.roll(part, 64, 1) * sine
            for i in range(per):
                first = (h // group) * positions * group + (c * per + i) * group + h % group
                rows[pl.ds(first, reqs, stride=row_count), :] = part[i * reqs : (i + 1) * reqs]
        return 0

    lax.fori_loop(0, chunks, combine, 0)
    for load in loads[4:]:
        load.wait()

    queries = positions * group
    lane = lax.broadcasted_iota(jnp.int32, (queries, context + 16), 1)
    at = lax.broadcasted_iota(jnp.int32, (queries, context + 16), 0) >> log2(group)
    new_valid = (lane >= context) & (lane - context <= at)
    scaling = 128 ** (-0.5)

    def attend(r):
        old_valid = lane < jnp.minimum(len_ref[r], context)
        valid = old_valid | new_valid
        for g in range(kv):
            span = pl.ds(pl.multiple_of(r * row_count + g * queries, queries), queries)
            query = rows[span, :].astype(jnp.bfloat16)
            scores = nt_dot(query, keys[r, g]) * scaling
            scores = jnp.where(valid, scores, -jnp.inf)
            top = jnp.max(scores, axis=1, keepdims=True)
            weights = jnp.exp(scores - top)
            weights = weights / jnp.sum(weights, axis=1, keepdims=True)
            rows[span, :] = jnp.dot(
                weights.astype(jnp.bfloat16), values[r, g], preferred_element_type=jnp.float32
            )

    def attend_some(b, _):
        for i in range(4):
            attend(b * 4 + i)
        return 0

    lax.fori_loop(0, reqs // 4, attend_some, 0)

    def finish(p, _):
        for h in range(heads):
            first = (h // group) * positions * group + p * group + h % group
            part = rows[pl.ds(first, reqs, stride=row_count), :]
            out_ref[p, :, h * 128 : (h + 1) * 128] = part.astype(jnp.bfloat16)
        return 0

    lax.fori_loop(0, positions, finish, 0)

    for k in range(1, n):
        def drain(c, _):
            out_copy(c, k).wait_send()
            back_copy(c, k).wait_send()
            return 0

        lax.fori_loop(0, chunks, drain, 0)


def per_device(
    hidden,
    unrotated_queries,
    adapter_ids,
    adapter_home,
    reduce_matrices,
    expand_matrices,
    correction_gain_table,
    key_cache,
    value_cache,
    new_keys,
    new_values,
    cache_len,
):
    n = lax.axis_size("adapter")
    tensors = lax.axis_size("tensor")
    me = lax.axis_index("adapter")
    reqs, positions, width = hidden.shape
    slots_dev, _, rank = reduce_matrices.shape
    kv, context, head_dim = key_cache.shape[1:]
    assert rank == 64 and head_dim == 128 and slots_dev % 2 == 0
    cap = max(2, (2 * reqs + n - 1) // n)
    chunks = max(1, min(positions, positions * cap // 16))
    per = positions // chunks
    block = per * cap
    total = n * block
    matches = adapter_ids[:, None] == jnp.arange(adapter_home.shape[0], dtype=jnp.int32)[None, :]
    home_slot = jnp.sum(jnp.where(matches, adapter_home[None, :], 0), axis=1)
    hop = lax.rem(home_slot // slots_dev - me + n, n)
    local_slot = home_slot % slots_dev
    order = jnp.arange(reqs, dtype=jnp.int32)
    earlier = (hop[:, None] == hop[None, :]) & (order[None, :] < order[:, None])
    pos = hop * cap + jnp.sum(earlier.astype(jnp.int32), axis=1)
    pos = jnp.tile(pos, per)
    slot_row = jnp.tile(local_slot, per)[None, :]
    gain_row = jnp.repeat(correction_gain_table, rank)[None, :]

    half = head_dim // 2
    frequency = rope_theta ** (-2.0 * jnp.arange(half, dtype=jnp.float32) / head_dim)
    offsets = cache_len[None, :] + jnp.arange(positions, dtype=jnp.int32)[:, None]
    angles = offsets.astype(jnp.float32)[:, :, None] * frequency[None, None, :]
    cosine, sine = jnp.cos(angles), jnp.sin(angles)
    cosine = jnp.concatenate([cosine, cosine], axis=-1).reshape(positions * reqs, head_dim)
    sine = jnp.concatenate([-sine, sine], axis=-1).reshape(positions * reqs, head_dim)

    def by_position(array):
        return array.transpose(1, 0, 2).reshape(positions * reqs, width)

    def fresh(array):
        return jnp.pad(array.transpose(0, 2, 1, 3), ((0, 0), (0, 0), (0, 16 - positions), (0, 0)))

    down = reduce_matrices.transpose(0, 2, 1).reshape(slots_dev * rank, width)
    up = expand_matrices.reshape(slots_dev * rank, width)
    dims = (n, tensors, chunks, cap, reqs, positions, context)
    bf16, f32 = jnp.bfloat16, jnp.float32
    dma = pltpu.SemaphoreType.DMA
    vmem = pl.BlockSpec(memory_space=pltpu.VMEM)
    whole = pl.BlockSpec(memory_space=pl.ANY)
    attended = pl.pallas_call(
        functools.partial(kernel, dims),
        out_shape=jax.ShapeDtypeStruct((positions, reqs, width), bf16),
        in_specs=[pl.BlockSpec(memory_space=pltpu.SMEM)] + [vmem] * 4 + [whole] * 8 + [vmem] * 2,
        out_specs=vmem,
        scratch_shapes=[
            pltpu.VMEM((positions * reqs, width), bf16),
            pltpu.VMEM((positions * reqs, width), bf16),
            pltpu.VMEM(down.shape, bf16),
            pltpu.VMEM(up.shape, bf16),
            pltpu.VMEM((reqs, kv, context + 16, head_dim), bf16),
            pltpu.VMEM((reqs, kv, context + 16, head_dim), bf16),
            pltpu.VMEM((chunks, n, block, width), bf16),
            pltpu.VMEM((chunks, n, block, width), bf16),
            pltpu.VMEM((n, block, 128), jnp.int32),
            pltpu.VMEM((n, block, 128), jnp.int32),
            pltpu.VMEM((chunks, tensors, total // 2, 128), f32),
            pltpu.VMEM((chunks, n, block, width), bf16),
            pltpu.VMEM((chunks, n, block, width), bf16),
            pltpu.VMEM((reqs * positions * width // head_dim, head_dim), f32),
            dma((8,)),
            dma((chunks, n)),
            dma((chunks, n)),
            dma((n,)),
            dma((n,)),
            dma((chunks, tensors)),
            dma((chunks, tensors)),
            dma((chunks, n)),
            dma((chunks, n)),
        ],
        compiler_params=pltpu.CompilerParams(
            collective_id=0, has_side_effects=True, vmem_limit_bytes=56 * 1024 * 1024
        ),
        cost_estimate=pl.CostEstimate(flops=3 << 30, bytes_accessed=16 << 20, transcendentals=0),
    )(
        cache_len,
        pos[None, :],
        pos[:, None],
        slot_row,
        gain_row,
        by_position(hidden),
        by_position(unrotated_queries),
        down,
        up,
        key_cache,
        value_cache,
        fresh(new_keys),
        fresh(new_values),
        cosine,
        sine,
    )
    return attended.transpose(1, 0, 2)


def solution(mesh):
    in_specs = (
        P(("replica", "adapter"), None, "tensor"),
        P(("replica", "adapter"), None, "tensor"),
        P(("replica", "adapter")),
        P("replica"),
        P("adapter", "tensor", None),
        P("adapter", None, "tensor"),
        P("adapter"),
        P(("replica", "adapter"), "tensor", None, None),
        P(("replica", "adapter"), "tensor", None, None),
        P(("replica", "adapter"), None, "tensor", None),
        P(("replica", "adapter"), None, "tensor", None),
        P(("replica", "adapter")),
    )
    out_specs = P(("replica", "adapter"), None, "tensor")
    return jax.shard_map(
        per_device, mesh=mesh, in_specs=in_specs, out_specs=out_specs, check_vma=False
    )
```

```python
import functools

import jax
import jax.numpy as jnp
from jax import lax
from jax.experimental import pallas as pl
from jax.experimental.pallas import tpu as pltpu
from jax.sharding import PartitionSpec as P

rope_theta = 500000.0
MESH = pl.DeviceIdType.MESH


def nt_dot(a, b):
    return lax.dot_general(a, b, (((1,), (1,)), ((), ())), preferred_element_type=jnp.float32)


def log2(n):
    bits = n.bit_length() - 1
    assert 1 << bits == n
    return bits


def kernel(
    dims,
    len_ref,
    pos_ref,
    pos_col_ref,
    slot_ref,
    gain_ref,
    hidden_hbm,
    uq_hbm,
    down_hbm,
    up_hbm,
    key_hbm,
    value_hbm,
    fresh_key_hbm,
    fresh_value_hbm,
    cos_ref,
    sin_ref,
    out_ref,
    hidden,
    uq,
    down,
    up,
    keys,
    values,
    outgoing,
    arrived,
    labels_out,
    labels_in,
    partial,
    returning,
    returned,
    rows,
    local_sems,
    out_send,
    out_recv,
    label_send,
    label_recv,
    part_send,
    part_recv,
    back_send,
    back_recv,
):
    n, tensors, chunks, cap, reqs, positions, context = dims
    per = positions // chunks
    block = per * cap
    total = n * block
    half = total // 2
    width = hidden.shape[-1]
    heads = width // 128
    kv = keys.shape[1]
    group = heads // kv
    row_count = positions * heads
    replica = lax.axis_index("replica")
    me = lax.axis_index("adapter")
    column = lax.axis_index("tensor")

    def adapter_peer(k):
        return (replica, lax.rem(me + k + n, n), column)

    def tensor_peer(k):
        return (replica, me, lax.rem(column + k, tensors))

    loads = [
        pltpu.make_async_copy(hidden_hbm, hidden, local_sems.at[0]),
        pltpu.make_async_copy(down_hbm, down, local_sems.at[1]),
        pltpu.make_async_copy(up_hbm, up, local_sems.at[2]),
        pltpu.make_async_copy(uq_hbm, uq, local_sems.at[3]),
        pltpu.make_async_copy(key_hbm, keys.at[:, :, pl.ds(0, context), :], local_sems.at[4]),
        pltpu.make_async_copy(value_hbm, values.at[:, :, pl.ds(0, context), :], local_sems.at[5]),
        pltpu.make_async_copy(
            fresh_key_hbm, keys.at[:, :, pl.ds(context, 16), :], local_sems.at[6]
        ),
        pltpu.make_async_copy(
            fresh_value_hbm, values.at[:, :, pl.ds(context, 16), :], local_sems.at[7]
        ),
    ]
    for load in loads:
        load.start()

    barrier = pltpu.get_barrier_semaphore()
    for k in range(1, n):
        pl.semaphore_signal(barrier, inc=1, device_id=adapter_peer(k), device_id_type=MESH)
    for k in range(1, tensors):
        pl.semaphore_signal(barrier, inc=1, device_id=tensor_peer(k), device_id_type=MESH)

    def out_copy(c, k):
        return pltpu.make_async_remote_copy(
            outgoing.at[c, k], arrived.at[c, k], out_send.at[c, k], out_recv.at[c, k],
            device_id=adapter_peer(k), device_id_type=MESH,
        )

    def label_copy(k):
        return pltpu.make_async_remote_copy(
            labels_out.at[k], labels_in.at[k], label_send.at[k], label_recv.at[k],
            device_id=adapter_peer(k), device_id_type=MESH,
        )

    def part_copy(c, k):
        return pltpu.make_async_remote_copy(
            partial.at[c, 0], partial.at[c, k], part_send.at[c, k], part_recv.at[c, k],
            device_id=tensor_peer(k), device_id_type=MESH,
        )

    def back_copy(c, k):
        return pltpu.make_async_remote_copy(
            returning.at[c, k], returned.at[c, k], back_send.at[c, k], back_recv.at[c, k],
            device_id=adapter_peer(-k), device_id_type=MESH,
        )

    def pick(shape, row_axis, pos):
        row = lax.broadcasted_iota(jnp.int32, shape, row_axis)
        col = lax.broadcasted_iota(jnp.int32, shape, 1 - row_axis)
        peer = row >> log2(block)
        row_pos = (row >> log2(cap)) & (per - 1)
        slot = row & (cap - 1)
        return (pos == peer * cap + slot) & (row_pos == (col >> log2(reqs)))

    forward = pick((total, per * reqs), 0, pos_ref[...])
    label_rows = jnp.sum(jnp.where(forward, slot_ref[...], 0), axis=1, keepdims=True)
    label_rows = jnp.broadcast_to(label_rows, (total, 128)).reshape(n, block, 128)
    labels_out[...] = label_rows
    labels_in[0] = label_rows[0]
    forward = jnp.where(forward, 1.0, 0.0).astype(jnp.bfloat16)

    loads[0].wait()
    pl.semaphore_wait(barrier, n - 1 + tensors - 1)
    for k in range(1, n):
        label_copy(k).start()

    def dispatch(c, _):
        source = hidden[pl.ds(pl.multiple_of(c * per * reqs, per * reqs), per * reqs), :]
        sent = jnp.dot(forward, source, preferred_element_type=jnp.float32)
        sent = sent.astype(jnp.bfloat16).reshape(n, block, width)
        outgoing[c] = sent
        arrived[c, 0] = sent[0]
        for k in range(1, n):
            out_copy(c, k).start()
        return 0

    lax.fori_loop(0, chunks, dispatch, 0)
    for k in range(1, n):
        label_copy(k).wait()
    loads[1].wait()
    loads[2].wait()

    def work(c, _):
        for k in range(1, n):
            out_copy(c, k).wait_recv()
        label = labels_in[...].reshape(total, 128)
        lane = lax.broadcasted_iota(jnp.int32, (total, 128), 1)
        odd = jnp.where(lane >= 64, 1, 0)
        product = nt_dot(arrived[c].reshape(total, width), down[...])
        kept = jnp.zeros((total, 128), jnp.float32)
        groups = down.shape[0] // 128
        for j in range(groups):
            kept = kept + jnp.where(label == 2 * j + odd, product[:, j * 128 : (j + 1) * 128], 0.0)
        kept = kept + pltpu.roll(kept, 64, 1)
        low = lax.broadcasted_iota(jnp.int32, (half, 128), 1) < 64
        partial[c, 0] = jnp.where(low, kept[:half], kept[half:])
        for k in range(1, tensors):
            part_copy(c, k).start()
        for k in range(1, tensors):
            part_copy(c, k).wait()
        summed = partial[c, 0]
        for k in range(1, tensors):
            summed = summed + partial[c, k]
        turned = pltpu.roll(summed, 64, 1)
        both = jnp.concatenate(
            [jnp.where(low, summed, turned), jnp.where(low, turned, summed)], axis=0
        )
        pieces = []
        for j in range(groups):
            scaled = both * gain_ref[:, j * 128 : (j + 1) * 128]
            pieces.append(jnp.where(label == 2 * j + odd, scaled, 0.0).astype(jnp.bfloat16))
        shrunk = jnp.concatenate(pieces, axis=1)
        expanded = jnp.dot(shrunk, up[...], preferred_element_type=jnp.float32)
        expanded = expanded.astype(jnp.bfloat16).reshape(n, block, width)
        returning[c] = expanded
        returned[c, 0] = expanded[0]
        for k in range(1, n):
            back_copy(c, k).start()
        return 0

    lax.fori_loop(0, chunks, work, 0)

    backward = pick((per * reqs, total), 1, pos_col_ref[...])
    backward = jnp.where(backward, 1.0, 0.0).astype(jnp.bfloat16)
    loads[3].wait()

    def combine(c, _):
        for k in range(1, n):
            back_copy(c, k).wait_recv()
        span = pl.ds(pl.multiple_of(c * per * reqs, per * reqs), per * reqs)
        delta = jnp.dot(
            backward, returned[c].reshape(total, width), preferred_element_type=jnp.float32
        )
        merged = uq[span, :].astype(jnp.float32) + delta
        cosine = cos_ref[span, :]
        sine = sin_ref[span, :]
        for h in range(heads):
            part = merged[:, h * 128 : (h + 1) * 128]
            part = part * cosine + pltpu.roll(part, 64, 1) * sine
            for i in range(per):
                first = (h // group) * positions * group + (c * per + i) * group + h % group
                rows[pl.ds(first, reqs, stride=row_count), :] = part[i * reqs : (i + 1) * reqs]
        return 0

    lax.fori_loop(0, chunks, combine, 0)
    for load in loads[4:]:
        load.wait()

    queries = positions * group
    lane = lax.broadcasted_iota(jnp.int32, (queries, context + 16), 1)
    at = lax.broadcasted_iota(jnp.int32, (queries, context + 16), 0) >> log2(group)
    new_valid = (lane >= context) & (lane - context <= at)
    scaling = 128 ** (-0.5)

    together = 4

    def attend(b, _):
        pairs = [(b * together + i, g) for i in range(together) for g in range(kv)]
        spans = [
            pl.ds(pl.multiple_of(r * row_count + g * queries, queries), queries) for r, g in pairs
        ]
        valid = [
            (lane < jnp.minimum(len_ref[b * together + i], context)) | new_valid
            for i in range(together)
        ]
        scores = [
            nt_dot(rows[span, :].astype(jnp.bfloat16), keys[r, g])
            for span, (r, g) in zip(spans, pairs)
        ]
        scores = [
            jnp.where(valid[i // kv], score * scaling, -jnp.inf) for i, score in enumerate(scores)
        ]
        tops = [jnp.max(score, axis=1, keepdims=True) for score in scores]
        weights = [jnp.exp(score - top) for score, top in zip(scores, tops)]
        sums = [jnp.sum(weight, axis=1, keepdims=True) for weight in weights]
        weights = [(weight / s).astype(jnp.bfloat16) for weight, s in zip(weights, sums)]
        results = [
            jnp.dot(weight, values[r, g], preferred_element_type=jnp.float32)
            for weight, (r, g) in zip(weights, pairs)
        ]
        for span, result in zip(spans, results):
            rows[span, :] = result
        return 0

    lax.fori_loop(0, reqs // together, attend, 0)

    def finish(p, _):
        for h in range(heads):
            first = (h // group) * positions * group + p * group + h % group
            part = rows[pl.ds(first, reqs, stride=row_count), :]
            out_ref[p, :, h * 128 : (h + 1) * 128] = part.astype(jnp.bfloat16)
        return 0

    lax.fori_loop(0, positions, finish, 0)

    for k in range(1, n):
        def drain(c, _):
            out_copy(c, k).wait_send()
            back_copy(c, k).wait_send()
            return 0

        lax.fori_loop(0, chunks, drain, 0)


def per_device(
    hidden,
    unrotated_queries,
    adapter_ids,
    adapter_home,
    reduce_matrices,
    expand_matrices,
    correction_gain_table,
    key_cache,
    value_cache,
    new_keys,
    new_values,
    cache_len,
):
    n = lax.axis_size("adapter")
    tensors = lax.axis_size("tensor")
    me = lax.axis_index("adapter")
    reqs, positions, width = hidden.shape
    slots_dev, _, rank = reduce_matrices.shape
    kv, context, head_dim = key_cache.shape[1:]
    assert rank == 64 and head_dim == 128 and slots_dev % 2 == 0
    cap = max(2, (2 * reqs + n - 1) // n)
    chunks = max(1, min(positions, positions * cap // 16))
    per = positions // chunks
    block = per * cap
    total = n * block
    matches = adapter_ids[:, None] == jnp.arange(adapter_home.shape[0], dtype=jnp.int32)[None, :]
    home_slot = jnp.sum(jnp.where(matches, adapter_home[None, :], 0), axis=1)
    hop = lax.rem(home_slot // slots_dev - me + n, n)
    local_slot = home_slot % slots_dev
    order = jnp.arange(reqs, dtype=jnp.int32)
    earlier = (hop[:, None] == hop[None, :]) & (order[None, :] < order[:, None])
    pos = hop * cap + jnp.sum(earlier.astype(jnp.int32), axis=1)
    pos = jnp.tile(pos, per)
    slot_row = jnp.tile(local_slot, per)[None, :]
    gain_row = jnp.repeat(correction_gain_table, rank)[None, :]

    half = head_dim // 2
    frequency = rope_theta ** (-2.0 * jnp.arange(half, dtype=jnp.float32) / head_dim)
    offsets = cache_len[None, :] + jnp.arange(positions, dtype=jnp.int32)[:, None]
    angles = offsets.astype(jnp.float32)[:, :, None] * frequency[None, None, :]
    cosine, sine = jnp.cos(angles), jnp.sin(angles)
    cosine = jnp.concatenate([cosine, cosine], axis=-1).reshape(positions * reqs, head_dim)
    sine = jnp.concatenate([-sine, sine], axis=-1).reshape(positions * reqs, head_dim)

    def by_position(array):
        return array.transpose(1, 0, 2).reshape(positions * reqs, width)

    def fresh(array):
        return jnp.pad(array.transpose(0, 2, 1, 3), ((0, 0), (0, 0), (0, 16 - positions), (0, 0)))

    down = reduce_matrices.transpose(0, 2, 1).reshape(slots_dev * rank, width)
    up = expand_matrices.reshape(slots_dev * rank, width)
    dims = (n, tensors, chunks, cap, reqs, positions, context)
    bf16, f32 = jnp.bfloat16, jnp.float32
    dma = pltpu.SemaphoreType.DMA
    vmem = pl.BlockSpec(memory_space=pltpu.VMEM)
    whole = pl.BlockSpec(memory_space=pl.ANY)
    attended = pl.pallas_call(
        functools.partial(kernel, dims),
        out_shape=jax.ShapeDtypeStruct((positions, reqs, width), bf16),
        in_specs=[pl.BlockSpec(memory_space=pltpu.SMEM)] + [vmem] * 4 + [whole] * 8 + [vmem] * 2,
        out_specs=vmem,
        scratch_shapes=[
            pltpu.VMEM((positions * reqs, width), bf16),
            pltpu.VMEM((positions * reqs, width), bf16),
            pltpu.VMEM(down.shape, bf16),
            pltpu.VMEM(up.shape, bf16),
            pltpu.VMEM((reqs, kv, context + 16, head_dim), bf16),
            pltpu.VMEM((reqs, kv, context + 16, head_dim), bf16),
            pltpu.VMEM((chunks, n, block, width), bf16),
            pltpu.VMEM((chunks, n, block, width), bf16),
            pltpu.VMEM((n, block, 128), jnp.int32),
            pltpu.VMEM((n, block, 128), jnp.int32),
            pltpu.VMEM((chunks, tensors, total // 2, 128), f32),
            pltpu.VMEM((chunks, n, block, width), bf16),
            pltpu.VMEM((chunks, n, block, width), bf16),
            pltpu.VMEM((reqs * positions * width // head_dim, head_dim), f32),
            dma((8,)),
            dma((chunks, n)),
            dma((chunks, n)),
            dma((n,)),
            dma((n,)),
            dma((chunks, tensors)),
            dma((chunks, tensors)),
            dma((chunks, n)),
            dma((chunks, n)),
        ],
        compiler_params=pltpu.CompilerParams(
            collective_id=0, has_side_effects=True, vmem_limit_bytes=56 * 1024 * 1024
        ),
        cost_estimate=pl.CostEstimate(flops=3 << 30, bytes_accessed=16 << 20, transcendentals=0),
    )(
        cache_len,
        pos[None, :],
        pos[:, None],
        slot_row,
        gain_row,
        by_position(hidden),
        by_position(unrotated_queries),
        down,
        up,
        key_cache,
        value_cache,
        fresh(new_keys),
        fresh(new_values),
        cosine,
        sine,
    )
    return attended.transpose(1, 0, 2)


def solution(mesh):
    in_specs = (
        P(("replica", "adapter"), None, "tensor"),
        P(("replica", "adapter"), None, "tensor"),
        P(("replica", "adapter")),
        P("replica"),
        P("adapter", "tensor", None),
        P("adapter", None, "tensor"),
        P("adapter"),
        P(("replica", "adapter"), "tensor", None, None),
        P(("replica", "adapter"), "tensor", None, None),
        P(("replica", "adapter"), None, "tensor", None),
        P(("replica", "adapter"), None, "tensor", None),
        P(("replica", "adapter")),
    )
    out_specs = P(("replica", "adapter"), None, "tensor")
    return jax.shard_map(
        per_device, mesh=mesh, in_specs=in_specs, out_specs=out_specs, check_vma=False
    )
```

```python
import functools

import jax
import jax.numpy as jnp
from jax import lax
from jax.experimental import pallas as pl
from jax.experimental.pallas import tpu as pltpu
from jax.sharding import PartitionSpec as P

rope_theta = 500000.0
MESH = pl.DeviceIdType.MESH


def nt_dot(a, b):
    return lax.dot_general(a, b, (((1,), (1,)), ((), ())), preferred_element_type=jnp.float32)


def log2(n):
    bits = n.bit_length() - 1
    assert 1 << bits == n
    return bits


def kernel(
    dims,
    len_ref,
    gain_ref,
    ids_ref,
    home_ref,
    len_row_ref,
    frequency_ref,
    hidden_hbm,
    uq_hbm,
    down_hbm,
    up_hbm,
    key_hbm,
    value_hbm,
    fresh_key_hbm,
    fresh_value_hbm,
    out_ref,
    hidden,
    uq,
    uq_rows,
    cosines,
    sines,
    down,
    up,
    keys,
    values,
    outgoing,
    arrived,
    labels_out,
    labels_in,
    partial,
    returning,
    returned,
    rows,
    local_sems,
    out_send,
    out_recv,
    label_send,
    label_recv,
    part_send,
    part_recv,
    back_send,
    back_recv,
):
    n, tensors, chunks, cap, reqs, positions, context, slots_dev = dims
    per = positions // chunks
    block = per * cap
    total = n * block
    half = total // 2
    width = hidden.shape[-1]
    heads = width // 128
    kv = keys.shape[1]
    group = heads // kv
    row_count = positions * heads
    replica = lax.axis_index("replica")
    me = lax.axis_index("adapter")
    column = lax.axis_index("tensor")

    def adapter_peer(k):
        return (replica, lax.rem(me + k + n, n), column)

    def tensor_peer(k):
        return (replica, me, lax.rem(column + k, tensors))

    loads = [
        pltpu.make_async_copy(hidden_hbm, hidden, local_sems.at[0]),
        pltpu.make_async_copy(down_hbm, down, local_sems.at[1]),
        pltpu.make_async_copy(up_hbm, up, local_sems.at[2]),
        pltpu.make_async_copy(uq_hbm, uq, local_sems.at[3]),
        pltpu.make_async_copy(key_hbm, keys.at[:, :, pl.ds(0, context), :], local_sems.at[4]),
        pltpu.make_async_copy(value_hbm, values.at[:, :, pl.ds(0, context), :], local_sems.at[5]),
    ]
    for g in range(kv):
        for i, (fresh_hbm, cache) in enumerate(((fresh_key_hbm, keys), (fresh_value_hbm, values))):
            loads.append(
                pltpu.make_async_copy(
                    fresh_hbm, cache.at[:, g, pl.ds(context, 16), :], local_sems.at[6 + 2 * g + i]
                )
            )
    for load in loads:
        load.start()

    barrier = pltpu.get_barrier_semaphore()
    for k in range(1, n):
        pl.semaphore_signal(barrier, inc=1, device_id=adapter_peer(k), device_id_type=MESH)
    for k in range(1, tensors):
        pl.semaphore_signal(barrier, inc=1, device_id=tensor_peer(k), device_id_type=MESH)

    def out_copy(c, k):
        return pltpu.make_async_remote_copy(
            outgoing.at[c, k], arrived.at[c, k], out_send.at[c, k], out_recv.at[c, k],
            device_id=adapter_peer(k), device_id_type=MESH,
        )

    def label_copy(k):
        return pltpu.make_async_remote_copy(
            labels_out.at[k], labels_in.at[k], label_send.at[k], label_recv.at[k],
            device_id=adapter_peer(k), device_id_type=MESH,
        )

    def part_copy(c, k):
        return pltpu.make_async_remote_copy(
            partial.at[c, 0], partial.at[c, k], part_send.at[c, k], part_recv.at[c, k],
            device_id=tensor_peer(k), device_id_type=MESH,
        )

    def back_copy(c, k):
        return pltpu.make_async_remote_copy(
            returning.at[c, k], returned.at[c, k], back_send.at[c, k], back_recv.at[c, k],
            device_id=adapter_peer(-k), device_id_type=MESH,
        )

    def pick(shape, row_axis, pos):
        row = lax.broadcasted_iota(jnp.int32, shape, row_axis)
        col = lax.broadcasted_iota(jnp.int32, shape, 1 - row_axis)
        peer = row >> log2(block)
        row_pos = (row >> log2(cap)) & (per - 1)
        slot = row & (cap - 1)
        return (pos == peer * cap + slot) & (row_pos == (col >> log2(reqs)))

    def as_column(row):
        size = row.shape[1]
        down_axis = lax.broadcasted_iota(jnp.int32, (size, size), 0)
        diagonal = down_axis == lax.broadcasted_iota(jnp.int32, (size, size), 1)
        return jnp.sum(jnp.where(diagonal, row, 0), axis=1, keepdims=True)

    span = per * reqs
    home_column = as_column(home_ref[...])
    table = lax.broadcasted_iota(jnp.int32, (home_column.shape[0], span), 0)
    home_slot = jnp.sum(jnp.where(table == ids_ref[...], home_column, 0), axis=0, keepdims=True)
    hop = ((home_slot >> log2(slots_dev)) - me + n) & (n - 1)
    local_slot = home_slot & (slots_dev - 1)
    other = lax.broadcasted_iota(jnp.int32, (span, span), 0)
    this = lax.broadcasted_iota(jnp.int32, (span, span), 1) & (reqs - 1)
    earlier = (as_column(hop) == hop) & (other < this)
    pos = hop * cap + jnp.sum(jnp.where(earlier, 1, 0), axis=0, keepdims=True)

    forward = pick((total, span), 0, pos)
    label_rows = jnp.sum(jnp.where(forward, local_slot, 0), axis=1, keepdims=True)
    label_rows = jnp.broadcast_to(label_rows, (total, 128)).reshape(n, block, 128)
    labels_out[...] = label_rows
    labels_in[0] = label_rows[0]
    forward = jnp.where(forward, 1.0, 0.0).astype(jnp.bfloat16)

    loads[0].wait()
    pl.semaphore_wait(barrier, n - 1 + tensors - 1)
    for k in range(1, n):
        label_copy(k).start()

    def position_rows(ref, c):
        pieces = [ref[:, c * per + i, :] for i in range(per)]
        return pieces[0] if per == 1 else jnp.concatenate(pieces, axis=0)

    for c in range(chunks):
        sent = jnp.dot(forward, position_rows(hidden, c), preferred_element_type=jnp.float32)
        sent = sent.astype(jnp.bfloat16).reshape(n, block, width)
        outgoing[c] = sent
        arrived[c, 0] = sent[0]
        for k in range(1, n):
            out_copy(c, k).start()

    backward = pick((span, total), 1, as_column(pos))
    backward = jnp.where(backward, 1.0, 0.0).astype(jnp.bfloat16)
    lengths = as_column(len_row_ref[...])
    low_half = lax.broadcasted_iota(jnp.int32, (reqs, 128), 1) < 64
    for p in range(positions):
        angles = (lengths + p).astype(jnp.float32) * frequency_ref[...]
        cosines[pl.ds(p * reqs, reqs), :] = jnp.cos(angles)
        sine = jnp.sin(angles)
        sines[pl.ds(p * reqs, reqs), :] = jnp.where(low_half, -sine, sine)
    loads[3].wait()
    for c in range(chunks):
        uq_rows[pl.ds(c * span, span), :] = position_rows(uq, c)
    for k in range(1, n):
        label_copy(k).wait()
    loads[1].wait()
    loads[2].wait()

    def work(c, _):
        for k in range(1, n):
            out_copy(c, k).wait_recv()
        label = labels_in[...].reshape(total, 128)
        lane = lax.broadcasted_iota(jnp.int32, (total, 128), 1)
        odd = jnp.where(lane >= 64, 1, 0)
        product = nt_dot(arrived[c].reshape(total, width), down[...])
        kept = jnp.zeros((total, 128), jnp.float32)
        groups = down.shape[0] // 128
        for j in range(groups):
            kept = kept + jnp.where(label == 2 * j + odd, product[:, j * 128 : (j + 1) * 128], 0.0)
        kept = kept + pltpu.roll(kept, 64, 1)
        low = lax.broadcasted_iota(jnp.int32, (half, 128), 1) < 64
        partial[c, 0] = jnp.where(low, kept[:half], kept[half:])
        for k in range(1, tensors):
            part_copy(c, k).start()
        for k in range(1, tensors):
            part_copy(c, k).wait()
        summed = partial[c, 0]
        for k in range(1, tensors):
            summed = summed + partial[c, k]
        turned = pltpu.roll(summed, 64, 1)
        both = jnp.concatenate(
            [jnp.where(low, summed, turned), jnp.where(low, turned, summed)], axis=0
        )
        pieces = []
        for j in range(groups):
            scaled = both * jnp.where(lane >= 64, gain_ref[2 * j + 1], gain_ref[2 * j])
            pieces.append(jnp.where(label == 2 * j + odd, scaled, 0.0).astype(jnp.bfloat16))
        shrunk = jnp.concatenate(pieces, axis=1)
        expanded = jnp.dot(shrunk, up[...], preferred_element_type=jnp.float32)
        expanded = expanded.astype(jnp.bfloat16).reshape(n, block, width)
        returning[c] = expanded
        returned[c, 0] = expanded[0]
        for k in range(1, n):
            back_copy(c, k).start()
        return 0

    lax.fori_loop(0, chunks, work, 0)

    def combine(c, _):
        for k in range(1, n):
            back_copy(c, k).wait_recv()
        part_rows = pl.ds(pl.multiple_of(c * span, span), span)
        delta = jnp.dot(
            backward, returned[c].reshape(total, width), preferred_element_type=jnp.float32
        )
        merged = uq_rows[part_rows, :].astype(jnp.float32) + delta
        cosine = cosines[part_rows, :]
        sine = sines[part_rows, :]
        for h in range(heads):
            part = merged[:, h * 128 : (h + 1) * 128]
            part = part * cosine + pltpu.roll(part, 64, 1) * sine
            for i in range(per):
                first = (h // group) * positions * group + (c * per + i) * group + h % group
                rows[pl.ds(first, reqs, stride=row_count), :] = part[i * reqs : (i + 1) * reqs]
        return 0

    lax.fori_loop(0, chunks, combine, 0)
    for load in loads[4:]:
        load.wait()

    queries = positions * group
    lane = lax.broadcasted_iota(jnp.int32, (queries, context + 16), 1)
    at = lax.broadcasted_iota(jnp.int32, (queries, context + 16), 0) >> log2(group)
    new_at = (lane - context) >> log2(kv)
    new_head = (lane - context) & (kv - 1)
    new_valid = [(lane >= context) & (new_at <= at) & (new_head == g) for g in range(kv)]
    scaling = 128 ** (-0.5)

    together = 8

    def attend(b, _):
        pairs = [(b * together + i, g) for i in range(together) for g in range(kv)]
        spans = [
            pl.ds(pl.multiple_of(r * row_count + g * queries, queries), queries) for r, g in pairs
        ]
        valid = [
            (lane < jnp.minimum(len_ref[r], context)) | new_valid[g] for r, g in pairs
        ]
        scores = [
            nt_dot(rows[span, :].astype(jnp.bfloat16), keys[r, g])
            for span, (r, g) in zip(spans, pairs)
        ]
        scores = [
            jnp.where(valid[i], score * scaling, -jnp.inf) for i, score in enumerate(scores)
        ]
        tops = [jnp.max(score, axis=1, keepdims=True) for score in scores]
        weights = [jnp.exp(score - top) for score, top in zip(scores, tops)]
        sums = [jnp.sum(weight, axis=1, keepdims=True) for weight in weights]
        weights = [(weight / s).astype(jnp.bfloat16) for weight, s in zip(weights, sums)]
        results = [
            jnp.dot(weight, values[r, g], preferred_element_type=jnp.float32)
            for weight, (r, g) in zip(weights, pairs)
        ]
        for span, result in zip(spans, results):
            rows[span, :] = result
        return 0

    lax.fori_loop(0, reqs // together, attend, 0)

    def finish(p, _):
        for h in range(heads):
            first = (h // group) * positions * group + p * group + h % group
            part = rows[pl.ds(first, reqs, stride=row_count), :]
            out_ref[p, :, h * 128 : (h + 1) * 128] = part.astype(jnp.bfloat16)
        return 0

    lax.fori_loop(0, positions, finish, 0)

    for k in range(1, n):
        def drain(c, _):
            out_copy(c, k).wait_send()
            back_copy(c, k).wait_send()
            return 0

        lax.fori_loop(0, chunks, drain, 0)


def per_device(
    hidden,
    unrotated_queries,
    adapter_ids,
    adapter_home,
    reduce_matrices,
    expand_matrices,
    correction_gain_table,
    key_cache,
    value_cache,
    new_keys,
    new_values,
    cache_len,
):
    n = lax.axis_size("adapter")
    tensors = lax.axis_size("tensor")
    reqs, positions, width = hidden.shape
    slots_dev, _, rank = reduce_matrices.shape
    kv, context, head_dim = key_cache.shape[1:]
    assert rank == 64 and head_dim == 128 and slots_dev % 2 == 0
    cap = max(2, (2 * reqs + n - 1) // n)
    chunks = max(1, min(positions, positions * cap // 16))
    per = positions // chunks
    block = per * cap
    total = n * block
    half = head_dim // 2
    frequency = rope_theta ** (-2.0 * jnp.arange(half, dtype=jnp.float32) / head_dim)
    frequency = jnp.concatenate([frequency, frequency])[None, :]

    def fresh(array):
        return jnp.pad(
            array.reshape(reqs, positions * kv, head_dim), ((0, 0), (0, 16 - positions * kv), (0, 0))
        )

    down = reduce_matrices.transpose(0, 2, 1).reshape(slots_dev * rank, width)
    up = expand_matrices.reshape(slots_dev * rank, width)
    dims = (n, tensors, chunks, cap, reqs, positions, context, slots_dev)
    bf16, f32 = jnp.bfloat16, jnp.float32
    dma = pltpu.SemaphoreType.DMA
    vmem = pl.BlockSpec(memory_space=pltpu.VMEM)
    whole = pl.BlockSpec(memory_space=pl.ANY)
    attended = pl.pallas_call(
        functools.partial(kernel, dims),
        out_shape=jax.ShapeDtypeStruct((positions, reqs, width), bf16),
        in_specs=[pl.BlockSpec(memory_space=pltpu.SMEM)] * 2 + [vmem] * 4 + [whole] * 8,
        out_specs=vmem,
        scratch_shapes=[
            pltpu.VMEM((reqs, positions, width), bf16),
            pltpu.VMEM((reqs, positions, width), bf16),
            pltpu.VMEM((positions * reqs, width), bf16),
            pltpu.VMEM((positions * reqs, head_dim), f32),
            pltpu.VMEM((positions * reqs, head_dim), f32),
            pltpu.VMEM(down.shape, bf16),
            pltpu.VMEM(up.shape, bf16),
            pltpu.VMEM((reqs, kv, context + 16, head_dim), bf16),
            pltpu.VMEM((reqs, kv, context + 16, head_dim), bf16),
            pltpu.VMEM((chunks, n, block, width), bf16),
            pltpu.VMEM((chunks, n, block, width), bf16),
            pltpu.VMEM((n, block, 128), jnp.int32),
            pltpu.VMEM((n, block, 128), jnp.int32),
            pltpu.VMEM((chunks, tensors, total // 2, 128), f32),
            pltpu.VMEM((chunks, n, block, width), bf16),
            pltpu.VMEM((chunks, n, block, width), bf16),
            pltpu.VMEM((reqs * positions * width // head_dim, head_dim), f32),
            dma((6 + 2 * kv,)),
            dma((chunks, n)),
            dma((chunks, n)),
            dma((n,)),
            dma((n,)),
            dma((chunks, tensors)),
            dma((chunks, tensors)),
            dma((chunks, n)),
            dma((chunks, n)),
        ],
        compiler_params=pltpu.CompilerParams(
            collective_id=0, has_side_effects=True, vmem_limit_bytes=56 * 1024 * 1024
        ),
        cost_estimate=pl.CostEstimate(flops=3 << 30, bytes_accessed=16 << 20, transcendentals=0),
    )(
        cache_len,
        correction_gain_table,
        jnp.tile(adapter_ids, per)[None, :],
        adapter_home[None, :],
        cache_len[None, :],
        frequency,
        hidden,
        unrotated_queries,
        down,
        up,
        key_cache,
        value_cache,
        fresh(new_keys),
        fresh(new_values),
    )
    return attended.transpose(1, 0, 2)


def solution(mesh):
    in_specs = (
        P(("replica", "adapter"), None, "tensor"),
        P(("replica", "adapter"), None, "tensor"),
        P(("replica", "adapter")),
        P("replica"),
        P("adapter", "tensor", None),
        P("adapter", None, "tensor"),
        P("adapter"),
        P(("replica", "adapter"), "tensor", None, None),
        P(("replica", "adapter"), "tensor", None, None),
        P(("replica", "adapter"), None, "tensor", None),
        P(("replica", "adapter"), None, "tensor", None),
        P(("replica", "adapter")),
    )
    out_specs = P(("replica", "adapter"), None, "tensor")
    return jax.shard_map(
        per_device, mesh=mesh, in_specs=in_specs, out_specs=out_specs, check_vma=False
    )
```

```python
import functools

import jax
import jax.numpy as jnp
from jax import lax
from jax.experimental import pallas as pl
from jax.experimental.pallas import tpu as pltpu
from jax.sharding import PartitionSpec as P

rope_theta = 500000.0
MESH = pl.DeviceIdType.MESH


def nt_dot(a, b):
    return lax.dot_general(a, b, (((1,), (1,)), ((), ())), preferred_element_type=jnp.float32)


def log2(n):
    bits = n.bit_length() - 1
    assert 1 << bits == n
    return bits


def kernel(
    dims,
    len_ref,
    gain_ref,
    ids_ref,
    home_ref,
    len_row_ref,
    frequency_ref,
    hidden_hbm,
    uq_hbm,
    down_hbm,
    up_hbm,
    key_hbm,
    value_hbm,
    fresh_key_hbm,
    fresh_value_hbm,
    out_ref,
    hidden,
    uq,
    uq_rows,
    cosines,
    sines,
    down,
    up,
    keys,
    values,
    fresh_keys,
    fresh_values,
    outgoing,
    arrived,
    labels_out,
    labels_in,
    partial,
    returning,
    returned,
    rows,
    local_sems,
    out_send,
    out_recv,
    label_send,
    label_recv,
    part_send,
    part_recv,
    back_send,
    back_recv,
):
    n, tensors, chunks, cap, reqs, positions, context, slots_dev = dims
    per = positions // chunks
    block = per * cap
    total = n * block
    half = total // 2
    width = hidden.shape[-1]
    heads = width // 128
    kv = keys.shape[1]
    group = heads // kv
    row_count = positions * heads
    replica = lax.axis_index("replica")
    me = lax.axis_index("adapter")
    column = lax.axis_index("tensor")

    def adapter_peer(k):
        return (replica, lax.rem(me + k + n, n), column)

    def tensor_peer(k):
        return (replica, me, lax.rem(column + k, tensors))

    loads = [
        pltpu.make_async_copy(hidden_hbm, hidden, local_sems.at[0]),
        pltpu.make_async_copy(down_hbm, down, local_sems.at[1]),
        pltpu.make_async_copy(up_hbm, up, local_sems.at[2]),
        pltpu.make_async_copy(uq_hbm, uq, local_sems.at[3]),
        pltpu.make_async_copy(key_hbm, keys.at[:, :, pl.ds(0, context), :], local_sems.at[4]),
        pltpu.make_async_copy(value_hbm, values.at[:, :, pl.ds(0, context), :], local_sems.at[5]),
        pltpu.make_async_copy(fresh_key_hbm, fresh_keys, local_sems.at[6]),
        pltpu.make_async_copy(fresh_value_hbm, fresh_values, local_sems.at[7]),
    ]
    loads[0].start()

    barrier = pltpu.get_barrier_semaphore()
    for k in range(1, n):
        pl.semaphore_signal(barrier, inc=1, device_id=adapter_peer(k), device_id_type=MESH)
    for k in range(1, tensors):
        pl.semaphore_signal(barrier, inc=1, device_id=tensor_peer(k), device_id_type=MESH)

    def out_copy(c, k):
        return pltpu.make_async_remote_copy(
            outgoing.at[c, k], arrived.at[c, k], out_send.at[c, k], out_recv.at[c, k],
            device_id=adapter_peer(k), device_id_type=MESH,
        )

    def label_copy(k):
        return pltpu.make_async_remote_copy(
            labels_out.at[k], labels_in.at[k], label_send.at[k], label_recv.at[k],
            device_id=adapter_peer(k), device_id_type=MESH,
        )

    def part_copy(c, k):
        return pltpu.make_async_remote_copy(
            partial.at[c, 0], partial.at[c, k], part_send.at[c, k], part_recv.at[c, k],
            device_id=tensor_peer(k), device_id_type=MESH,
        )

    def back_copy(c, k):
        return pltpu.make_async_remote_copy(
            returning.at[c, k], returned.at[c, k], back_send.at[c, k], back_recv.at[c, k],
            device_id=adapter_peer(-k), device_id_type=MESH,
        )

    def pick(shape, row_axis, pos):
        row = lax.broadcasted_iota(jnp.int32, shape, row_axis)
        col = lax.broadcasted_iota(jnp.int32, shape, 1 - row_axis)
        peer = row >> log2(block)
        row_pos = (row >> log2(cap)) & (per - 1)
        slot = row & (cap - 1)
        return (pos == peer * cap + slot) & (row_pos == (col >> log2(reqs)))

    def as_column(row):
        size = row.shape[1]
        down_axis = lax.broadcasted_iota(jnp.int32, (size, size), 0)
        diagonal = down_axis == lax.broadcasted_iota(jnp.int32, (size, size), 1)
        return jnp.sum(jnp.where(diagonal, row, 0), axis=1, keepdims=True)

    span = per * reqs
    home_column = as_column(home_ref[...])
    table = lax.broadcasted_iota(jnp.int32, (home_column.shape[0], span), 0)
    home_slot = jnp.sum(jnp.where(table == ids_ref[...], home_column, 0), axis=0, keepdims=True)
    hop = ((home_slot >> log2(slots_dev)) - me + n) & (n - 1)
    local_slot = home_slot & (slots_dev - 1)
    other = lax.broadcasted_iota(jnp.int32, (span, span), 0)
    this = lax.broadcasted_iota(jnp.int32, (span, span), 1) & (reqs - 1)
    earlier = (as_column(hop) == hop) & (other < this)
    pos = hop * cap + jnp.sum(jnp.where(earlier, 1, 0), axis=0, keepdims=True)

    forward = pick((total, span), 0, pos)
    label_rows = jnp.sum(jnp.where(forward, local_slot, 0), axis=1, keepdims=True)
    label_rows = jnp.broadcast_to(label_rows, (total, 128)).reshape(n, block, 128)
    labels_out[...] = label_rows
    labels_in[0] = label_rows[0]
    forward = jnp.where(forward, 1.0, 0.0).astype(jnp.bfloat16)

    loads[0].wait()
    pl.semaphore_wait(barrier, n - 1 + tensors - 1)
    for k in range(1, n):
        label_copy(k).start()
    for load in loads[1:3]:
        load.start()

    def position_rows(ref, c):
        pieces = [ref[:, c * per + i, :] for i in range(per)]
        return pieces[0] if per == 1 else jnp.concatenate(pieces, axis=0)

    for c in range(chunks):
        sent = jnp.dot(forward, position_rows(hidden, c), preferred_element_type=jnp.float32)
        sent = sent.astype(jnp.bfloat16).reshape(n, block, width)
        outgoing[c] = sent
        arrived[c, 0] = sent[0]
        for k in range(1, n):
            out_copy(c, k).start()

    for load in loads[3:]:
        load.start()

    backward = pick((span, total), 1, as_column(pos))
    backward = jnp.where(backward, 1.0, 0.0).astype(jnp.bfloat16)
    lengths = as_column(len_row_ref[...])
    low_half = lax.broadcasted_iota(jnp.int32, (reqs, 128), 1) < 64
    for p in range(positions):
        angles = (lengths + p).astype(jnp.float32) * frequency_ref[...]
        cosines[pl.ds(p * reqs, reqs), :] = jnp.cos(angles)
        sine = jnp.sin(angles)
        sines[pl.ds(p * reqs, reqs), :] = jnp.where(low_half, -sine, sine)
    loads[3].wait()
    for c in range(chunks):
        uq_rows[pl.ds(c * span, span), :] = position_rows(uq, c)
    for load in loads[6:]:
        load.wait()
    for fresh, cache in ((fresh_keys, keys), (fresh_values, values)):
        given = fresh[...].astype(jnp.float32)
        blank = jnp.zeros((reqs, 16 - given.shape[1], 128), jnp.float32)
        padded = jnp.concatenate([given, blank], axis=1).astype(jnp.bfloat16)
        for g in range(kv):
            cache[:, g, context : context + 16, :] = padded
    for k in range(1, n):
        label_copy(k).wait()
    loads[1].wait()
    loads[2].wait()

    def work(c, _):
        for k in range(1, n):
            out_copy(c, k).wait_recv()

        @pl.when(c > 0)
        def _():
            for k in range(1, n):
                back_copy(c - 1, k).start()

        label = labels_in[...].reshape(total, 128)
        lane = lax.broadcasted_iota(jnp.int32, (total, 128), 1)
        odd = jnp.where(lane >= 64, 1, 0)
        product = nt_dot(arrived[c].reshape(total, width), down[...])
        kept = jnp.zeros((total, 128), jnp.float32)
        groups = down.shape[0] // 128
        for j in range(groups):
            kept = kept + jnp.where(label == 2 * j + odd, product[:, j * 128 : (j + 1) * 128], 0.0)
        kept = kept + pltpu.roll(kept, 64, 1)
        low = lax.broadcasted_iota(jnp.int32, (half, 128), 1) < 64
        partial[c, 0] = jnp.where(low, kept[:half], kept[half:])
        for k in range(1, tensors):
            part_copy(c, k).start()
        for k in range(1, tensors):
            part_copy(c, k).wait()
        summed = partial[c, 0]
        for k in range(1, tensors):
            summed = summed + partial[c, k]
        turned = pltpu.roll(summed, 64, 1)
        both = jnp.concatenate(
            [jnp.where(low, summed, turned), jnp.where(low, turned, summed)], axis=0
        )
        pieces = []
        for j in range(groups):
            scaled = both * jnp.where(lane >= 64, gain_ref[2 * j + 1], gain_ref[2 * j])
            pieces.append(jnp.where(label == 2 * j + odd, scaled, 0.0).astype(jnp.bfloat16))
        shrunk = jnp.concatenate(pieces, axis=1)
        expanded = jnp.dot(shrunk, up[...], preferred_element_type=jnp.float32)
        expanded = expanded.astype(jnp.bfloat16).reshape(n, block, width)
        returning[c] = expanded
        returned[c, 0] = expanded[0]
        return 0

    lax.fori_loop(0, chunks, work, 0)
    for k in range(1, n):
        back_copy(chunks - 1, k).start()

    def combine(c, _):
        for k in range(1, n):
            back_copy(c, k).wait_recv()
        part_rows = pl.ds(pl.multiple_of(c * span, span), span)
        delta = jnp.dot(
            backward, returned[c].reshape(total, width), preferred_element_type=jnp.float32
        )
        merged = uq_rows[part_rows, :].astype(jnp.float32) + delta
        cosine = cosines[part_rows, :]
        sine = sines[part_rows, :]
        for h in range(heads):
            part = merged[:, h * 128 : (h + 1) * 128]
            part = part * cosine + pltpu.roll(part, 64, 1) * sine
            for i in range(per):
                first = (h // group) * positions * group + (c * per + i) * group + h % group
                rows[pl.ds(first, reqs, stride=row_count), :] = part[i * reqs : (i + 1) * reqs]
        return 0

    def attend_positions(begin, end):
        queries = (end - begin) * group
        lane = lax.broadcasted_iota(jnp.int32, (queries, context + 16), 1)
        at = (lax.broadcasted_iota(jnp.int32, lane.shape, 0) >> log2(group)) + begin
        new_at = (lane - context) >> log2(kv)
        new_head = (lane - context) & (kv - 1)
        new_valid = [(lane >= context) & (new_at <= at) & (new_head == g) for g in range(kv)]
        scaling = 128 ** (-0.5)

        together = 8

        def attend(b, _):
            pairs = [(b * together + i, g) for i in range(together) for g in range(kv)]
            spans = [
                pl.ds(pl.multiple_of(r * row_count + (g * positions + begin) * group, group), queries) for r, g in pairs
            ]
            valid = [
                (lane < jnp.minimum(len_ref[r], context)) | new_valid[g] for r, g in pairs
            ]
            scores = [
                nt_dot(rows[span, :].astype(jnp.bfloat16), keys[r, g])
                for span, (r, g) in zip(spans, pairs)
            ]
            scores = [
                jnp.where(valid[i], score * scaling, -jnp.inf) for i, score in enumerate(scores)
            ]
            tops = [jnp.max(score, axis=1, keepdims=True) for score in scores]
            weights = [jnp.exp(score - top) for score, top in zip(scores, tops)]
            sums = [jnp.sum(weight, axis=1, keepdims=True) for weight in weights]
            weights = [(weight / s).astype(jnp.bfloat16) for weight, s in zip(weights, sums)]
            results = [
                jnp.dot(weight, values[r, g], preferred_element_type=jnp.float32)
                for weight, (r, g) in zip(weights, pairs)
            ]
            for span, result in zip(spans, results):
                rows[span, :] = result
            return 0

        lax.fori_loop(0, reqs // together, attend, 0)

    early = max(0, positions - 1) if chunks == positions else 0
    lax.fori_loop(0, early, combine, 0)
    for load in loads[4:6]:
        load.wait()
    if early:
        attend_positions(0, early)
    lax.fori_loop(early, chunks, combine, 0)
    attend_positions(early, positions)

    def finish(p, _):
        for h in range(heads):
            first = (h // group) * positions * group + p * group + h % group
            part = rows[pl.ds(first, reqs, stride=row_count), :]
            out_ref[p, :, h * 128 : (h + 1) * 128] = part.astype(jnp.bfloat16)
        return 0

    lax.fori_loop(0, positions, finish, 0)

    for k in range(1, n):
        def drain(c, _):
            out_copy(c, k).wait_send()
            back_copy(c, k).wait_send()
            return 0

        lax.fori_loop(0, chunks, drain, 0)


def per_device(
    hidden,
    unrotated_queries,
    adapter_ids,
    adapter_home,
    reduce_matrices,
    expand_matrices,
    correction_gain_table,
    key_cache,
    value_cache,
    new_keys,
    new_values,
    cache_len,
):
    n = lax.axis_size("adapter")
    tensors = lax.axis_size("tensor")
    reqs, positions, width = hidden.shape
    slots_dev, _, rank = reduce_matrices.shape
    kv, context, head_dim = key_cache.shape[1:]
    assert rank == 64 and head_dim == 128 and slots_dev % 2 == 0
    cap = max(2, (2 * reqs + n - 1) // n)
    chunks = max(1, min(positions, positions * cap // 16))
    per = positions // chunks
    block = per * cap
    total = n * block
    half = head_dim // 2
    frequency = rope_theta ** (-2.0 * jnp.arange(half, dtype=jnp.float32) / head_dim)
    frequency = jnp.concatenate([frequency, frequency])[None, :]

    def fresh(array):
        return array.reshape(reqs, positions * kv, head_dim)

    down = reduce_matrices.transpose(0, 2, 1).reshape(slots_dev * rank, width)
    up = expand_matrices.reshape(slots_dev * rank, width)
    dims = (n, tensors, chunks, cap, reqs, positions, context, slots_dev)
    bf16, f32 = jnp.bfloat16, jnp.float32
    dma = pltpu.SemaphoreType.DMA
    vmem = pl.BlockSpec(memory_space=pltpu.VMEM)
    whole = pl.BlockSpec(memory_space=pl.ANY)
    attended = pl.pallas_call(
        functools.partial(kernel, dims),
        out_shape=jax.ShapeDtypeStruct((positions, reqs, width), bf16),
        in_specs=[pl.BlockSpec(memory_space=pltpu.SMEM)] * 2 + [vmem] * 4 + [whole] * 8,
        out_specs=vmem,
        scratch_shapes=[
            pltpu.VMEM((reqs, positions, width), bf16),
            pltpu.VMEM((reqs, positions, width), bf16),
            pltpu.VMEM((positions * reqs, width), bf16),
            pltpu.VMEM((positions * reqs, head_dim), f32),
            pltpu.VMEM((positions * reqs, head_dim), f32),
            pltpu.VMEM(down.shape, bf16),
            pltpu.VMEM(up.shape, bf16),
            pltpu.VMEM((reqs, kv, context + 16, head_dim), bf16),
            pltpu.VMEM((reqs, kv, context + 16, head_dim), bf16),
            pltpu.VMEM((reqs, positions * kv, head_dim), bf16),
            pltpu.VMEM((reqs, positions * kv, head_dim), bf16),
            pltpu.VMEM((chunks, n, block, width), bf16),
            pltpu.VMEM((chunks, n, block, width), bf16),
            pltpu.VMEM((n, block, 128), jnp.int32),
            pltpu.VMEM((n, block, 128), jnp.int32),
            pltpu.VMEM((chunks, tensors, total // 2, 128), f32),
            pltpu.VMEM((chunks, n, block, width), bf16),
            pltpu.VMEM((chunks, n, block, width), bf16),
            pltpu.VMEM((reqs * positions * width // head_dim, head_dim), f32),
            dma((8,)),
            dma((chunks, n)),
            dma((chunks, n)),
            dma((n,)),
            dma((n,)),
            dma((chunks, tensors)),
            dma((chunks, tensors)),
            dma((chunks, n)),
            dma((chunks, n)),
        ],
        compiler_params=pltpu.CompilerParams(
            collective_id=0, has_side_effects=True, vmem_limit_bytes=56 * 1024 * 1024
        ),
        cost_estimate=pl.CostEstimate(flops=3 << 30, bytes_accessed=16 << 20, transcendentals=0),
    )(
        cache_len,
        correction_gain_table,
        jnp.tile(adapter_ids, per)[None, :],
        adapter_home[None, :],
        cache_len[None, :],
        frequency,
        hidden,
        unrotated_queries,
        down,
        up,
        key_cache,
        value_cache,
        fresh(new_keys),
        fresh(new_values),
    )
    return attended.transpose(1, 0, 2)


def solution(mesh):
    in_specs = (
        P(("replica", "adapter"), None, "tensor"),
        P(("replica", "adapter"), None, "tensor"),
        P(("replica", "adapter")),
        P("replica"),
        P("adapter", "tensor", None),
        P("adapter", None, "tensor"),
        P("adapter"),
        P(("replica", "adapter"), "tensor", None, None),
        P(("replica", "adapter"), "tensor", None, None),
        P(("replica", "adapter"), None, "tensor", None),
        P(("replica", "adapter"), None, "tensor", None),
        P(("replica", "adapter")),
    )
    out_specs = P(("replica", "adapter"), None, "tensor")
    return jax.shard_map(
        per_device, mesh=mesh, in_specs=in_specs, out_specs=out_specs, check_vma=False
    )
```
